128 devices in a mesh: row: 16 (over z_hi, y, core), col: 8 (over x, z_lo).
Axes of the slice: x: 4, y: 4, z: 4 (z_hi: 2, z_lo: 2; z = z_hi * 2 + z_lo), core: 2. Of those that a mesh axis runs over, the one named last changes fastest.
Arguments:
- trial_vectors: bfloat16 [24576, 256], P(('row', 'col')), may hold values from -6 to 6
- h_blocks: bfloat16 [8, 16, 24, 64, 16, 128], P('col', None, None, None, 'row'), may hold values from -0.09375 to 0.09375
- block_col: int32 [8, 16, 24, 16, 2], P('col', 'row'), may hold values from 0 to 2
- block_count: int32 [8, 16, 24, 16], P('col', 'row'), may hold values from 0 to 2, as said below
- center: float32 [1], replicated, may hold values from -0.5 to 0.5
- half_width: float32 [1], replicated, may hold values from 1.5 to 2.5
Outputs:
- filtered: float32 [24576, 256], P(('row', 'col'))
The draws below stay inside these ranges and needn't reach their ends.
Inputs may be any that keep to these rules, and one draw needn't show every extreme that they name: Only the first block_count slots of a block row and source domain hold blocks. In every column group one row domain has all 2 slots used in every block row for every source domain.
All inputs are finite; a program needn't handle non-finite values.
Results may differ from the reference program's by a relative error of at most 0.019.
Values may be sent and summed in bfloat16 or wider, within the bound.
A program may use at most 64 MiB of HBM per device.

```python
import jax
import jax.numpy as jnp
from jax import lax

BLOCK = 64
VECTORS = 256
PER = 2
DEGREE = 6
BLOCK_ROWS = 3
DOMAIN_ROWS = 24
ORBITALS = 24576
N_ROW = 16
N_COL = 8


def draw_block_count(key, part):
    first, second = jax.random.split(jax.random.fold_in(key, 23))
    target = jnp.arange(N_ROW).astype(jnp.int32)[:, None, None]
    source = jnp.arange(N_ROW).astype(jnp.int32)[None, None, :]
    spacing = jnp.abs(target - source)
    apart = jnp.minimum(spacing, N_ROW - spacing)
    base = jax.random.randint(first, (N_COL, N_ROW, DOMAIN_ROWS, N_ROW), 0, PER + 1)
    counts = jnp.minimum(PER, base * 4 // (2 + apart))
    chosen = jax.random.randint(second, (N_COL, 1, 1, 1), 0, N_ROW)
    counts = jnp.where(target[None] == chosen, PER, counts)
    return counts.astype(jnp.int32)


def touch_ends(drawn, stream_key, least, top_value):
    longest = drawn.shape.index(max(drawn.shape))
    spots = []
    for shift in (0, 1):
        where = [jax.random.randint(jax.random.fold_in(stream_key, axis), (), 0, length) for axis, length in enumerate(drawn.shape)]
        where[longest] = (where[longest] + shift) % drawn.shape[longest]
        spots.append(tuple(where))
    return drawn.at[spots[0]].set(least).at[spots[1]].set(top_value)


def levels(own_key, extent, cuts, smallest, top_value):
    factor_of = 1.0
    for axis_at, parts in cuts:
        draws = jax.random.uniform(jax.random.fold_in(jax.random.fold_in(own_key, 6), axis_at), (parts,), jnp.float32, smallest / len(cuts), top_value / len(cuts))
        factor_of = factor_of * jnp.repeat(jnp.exp(draws), extent[axis_at] // parts).reshape((-1,) + (1,) * (len(extent) - 1 - axis_at))
    return factor_of


def scatter_about(key, extent, scale, reach, cuts=(), kind=jnp.bfloat16):
    array = jax.random.normal(key, extent, jnp.float32) * scale
    if len(cuts) > 0:
        array = levels(key, extent, cuts, -0.22, 0.18) * array
    return jnp.clip(array, min=-reach, max=reach).astype(kind)


def setup_inputs(seed: int = 0) -> dict:
    splits = jax.random.split(jax.random.key(seed), 7)
    trial_vectors = scatter_about(splits[0], (ORBITALS, VECTORS), 1.0, 6.0, ((0, 128),))
    h_blocks = scatter_about(splits[1], (N_COL, N_ROW, DOMAIN_ROWS, BLOCK, N_ROW, PER * BLOCK), (N_COL * N_ROW * PER * BLOCK // 4) ** -0.5, 0.09375, ((0, 8), (4, 16)))
    block_col = touch_ends(jax.random.randint(splits[2], (N_COL, N_ROW, DOMAIN_ROWS, N_ROW, PER), 0, BLOCK_ROWS), jax.random.fold_in(splits[2], 1), 0, BLOCK_ROWS - 1).astype(jnp.int32)
    block_count = draw_block_count(jax.random.fold_in(splits[6], 71), 0)
    center = jnp.clip(jax.random.uniform(splits[4], (1,), jnp.float32, -0.5, 0.5), -0.5, 0.5)
    half_width = jnp.clip(jax.random.uniform(splits[5], (1,), jnp.float32, 1.5, 2.5), 1.5, 2.5)
    return {"trial_vectors": trial_vectors, "h_blocks": h_blocks, "block_col": block_col, "block_count": block_count, "center": center, "half_width": half_width}


def apply_operator(panel, h_blocks, block_col, block_count):
    domain = BLOCK_ROWS * N_COL
    contraction = N_ROW * PER * BLOCK
    xblocks = lax.optimization_barrier(panel).reshape(N_ROW * domain, BLOCK, VECTORS)
    slot_index = jnp.arange(PER, dtype=jnp.int32)
    source_index = jnp.arange(N_ROW, dtype=jnp.int32)

    def one_domain(group_index, domain_index):
        filled = slot_index[None, None, :] < block_count[group_index, domain_index][:, :, None]
        raw_blocks = h_blocks[group_index, domain_index].reshape(domain, BLOCK, N_ROW, PER, BLOCK)
        masked = jnp.where(filled[:, None, :, :, None], raw_blocks, jnp.zeros((), raw_blocks.dtype))
        masked = masked.reshape(domain, BLOCK, contraction)
        columns = (source_index[None, :, None] * N_COL + group_index) * BLOCK_ROWS + block_col[group_index, domain_index]
        columns = columns.reshape(domain, N_ROW * PER).astype(jnp.int32)
        picked = xblocks[columns].reshape(domain, contraction, VECTORS)
        return jnp.einsum("rak,rkv->rav", masked.astype(jnp.float32), picked.astype(jnp.float32))

    def per_group(summed, group_index):
        sums = lax.map(lambda domain_index: one_domain(group_index, domain_index), jnp.arange(N_ROW, dtype=jnp.int32))
        rounded = lax.optimization_barrier(sums.astype(jnp.bfloat16))
        return summed + rounded.astype(jnp.float32), None

    summed, _ = lax.scan(per_group, jnp.zeros((N_ROW, domain, BLOCK, VECTORS), jnp.float32), jnp.arange(N_COL, dtype=jnp.int32))
    return summed.reshape(N_ROW * domain * BLOCK, VECTORS)


def reference(trial_vectors, h_blocks, block_col, block_count, center, half_width):
    centre_value = center[0]
    half_value = half_width[0]
    previous = trial_vectors.astype(jnp.float32)
    current = (apply_operator(trial_vectors, h_blocks, block_col, block_count) - centre_value * previous) / half_value
    for degree_step in range(DEGREE - 1):
        panel_now = current.astype(jnp.bfloat16)
        product = apply_operator(panel_now, h_blocks, block_col, block_count)
        following = 2.0 * (product - centre_value * current) / half_value - previous
        previous, current = current, following
    return current
```

```python
import jax
import jax.numpy as jnp
from jax import lax
from jax.experimental import pallas as pl
from jax.experimental.pallas import tpu as pltpu
from jax.sharding import PartitionSpec as P

BLOCK = 64
VECTORS = 256
PER = 2
DEGREE = 6
BLOCK_ROWS = 3
N_ROW = 16
N_COL = 8
OWN = BLOCK_ROWS * BLOCK
DOMAIN = BLOCK_ROWS * N_COL
ROWS = DOMAIN * BLOCK
CHUNKS = 4
CHUNK = 4 * OWN
MESH = pl.DeviceIdType.MESH


def flip(value):
    return value + 1 - 2 * (value % 2)


def kernel(
    coef_ref,
    scal_ref,
    trial_ref,
    h_ref,
    out_ref,
    hbuf,
    dense,
    gathered,
    total,
    partial,
    arrived,
    current,
    previous,
    h_send,
    h_recv,
    own_sem,
    g_send,
    f_send,
    g_recv,
    p_send,
    p_recv,
):
    row, col = lax.axis_index("row"), lax.axis_index("col")
    core, y, zh = row % 2, (row // 2) % 4, row // 8
    x, zl = col // 2, col % 2
    mate = flip(row)

    def pair_y(j):
        base = y if j < 2 else (y + 2) % 4
        return flip(base) if j % 2 else base

    chips = [(zh if m < 4 else 1 - zh, pair_y(m % 4)) for m in range(8)]
    same_core = [a * 8 + b * 2 + core for a, b in chips]
    other_core = [a * 8 + b * 2 + 1 - core for a, b in chips]
    cols = [((x + j) % 4) * 2 + k for j in range(4) for k in range(2)]

    barrier = pltpu.get_barrier_semaphore()
    row_peers = same_core[1:] + other_core
    for peer in row_peers:
        pl.semaphore_signal(barrier, inc=1, device_id=(peer, col), device_id_type=MESH)
    for j in range(1, N_COL):
        pl.semaphore_signal(
            barrier, inc=1, device_id=(row, (col + j) % N_COL), device_id_type=MESH
        )
    pl.semaphore_wait(barrier, len(row_peers) + N_COL - 1)

    def v_slot(p, s):
        return gathered.at[p, s // 4, pl.ds(pl.multiple_of((s % 4) * OWN, OWN), OWN), :]

    def v_copy(p, s, sem, to):
        return pltpu.make_async_remote_copy(
            src_ref=v_slot(p, s),
            dst_ref=v_slot(p, s),
            send_sem=sem,
            recv_sem=g_recv.at[p, s],
            device_id=(to, col),
            device_id_type=MESH,
        )

    def start_gather(p):
        v_copy(p, row, g_send.at[0], mate).start()
        for m in (1, 3, 2, 4, 5, 7, 6):
            v_copy(p, row, g_send.at[m], same_core[m]).start()

    current[...] = trial_ref[...].astype(jnp.float32)
    previous[...] = jnp.zeros_like(previous)
    gathered[0, row // 4, pl.ds(pl.multiple_of((row % 4) * OWN, OWN), OWN), :] = trial_ref[...]
    start_gather(0)

    def h_copy(i, to):
        return pltpu.make_async_remote_copy(
            src_ref=h_ref.at[to],
            dst_ref=hbuf.at[row],
            send_sem=h_send.at[i],
            recv_sem=h_recv.at[row],
            device_id=(to, col),
            device_id_type=MESH,
        )

    for i, peer in enumerate(row_peers):
        h_copy(i, peer).start()
    own = pltpu.make_async_copy(h_ref.at[row], hbuf.at[row], own_sem)
    own.start()
    own.wait()

    def h_wait(s):
        pltpu.make_async_remote_copy(
            src_ref=h_ref.at[0],
            dst_ref=hbuf.at[s],
            send_sem=h_send.at[0],
            recv_sem=h_recv.at[s],
            device_id=(mate, col),
            device_id_type=MESH,
        ).wait_recv()

    left = lax.broadcasted_iota(jnp.int32, (BLOCK, 2 * BLOCK), 1) < BLOCK

    def expand(pair):
        even, odd = pair * 2, pair * 2 + 1

        def one(i, carry):
            def coef(s, q, j):
                return coef_ref[((i * N_ROW + s) * PER + q) * BLOCK_ROWS + j]

            def lanes(a, b):
                return jnp.where(left, a, b)

            be = hbuf[even, i].astype(jnp.float32)
            bo = hbuf[odd, i].astype(jnp.float32)
            re, ro = pltpu.roll(be, BLOCK, 1), pltpu.roll(bo, BLOCK, 1)
            first = be * lanes(coef(even, 0, 0), coef(even, 1, 1)) + re * lanes(
                coef(even, 1, 0), coef(even, 0, 1)
            )
            middle = jnp.where(
                left,
                be * coef(even, 0, 2) + re * coef(even, 1, 2),
                bo * coef(odd, 1, 0) + ro * coef(odd, 0, 0),
            )
            last = bo * lanes(coef(odd, 0, 1), coef(odd, 1, 2)) + ro * lanes(
                coef(odd, 1, 1), coef(odd, 0, 2)
            )
            at = pl.ds(pl.multiple_of(i * BLOCK, BLOCK), BLOCK)
            offset = (pair % 2) * (2 * OWN)
            for k, part in enumerate((first, middle, last)):
                dense[
                    pair // 2,
                    at,
                    pl.ds(pl.multiple_of(offset + k * 2 * BLOCK, 2 * BLOCK), 2 * BLOCK),
                ] = part.astype(jnp.bfloat16)
            return carry

        lax.fori_loop(0, DOMAIN, one, 0)

    for m in range(8):
        if m > 0:
            h_wait(same_core[m])
        h_wait(other_core[m])
        expand(same_core[m] // 2)
    for i, peer in enumerate(row_peers):
        h_copy(i, peer).wait_send()

    center, half = scal_ref[0], scal_ref[1]
    TILE = 2 * OWN

    def step(k, carry):
        p = k % 2

        @pl.when(k > 0)
        def _():
            start_gather(p)

        def product(m, rows_at):
            chunk = same_core[2 * m] // 4
            return jnp.dot(
                dense[chunk, rows_at, :],
                gathered[p, chunk],
                preferred_element_type=jnp.float32,
            )

        for m in range(CHUNKS):
            for n in (2 * m, 2 * m + 1):
                if n > 0:
                    v_copy(p, same_core[n], f_send.at[n], mate).wait_recv()
                    v_copy(p, same_core[n], f_send.at[n], mate).start()
            for n in (2 * m, 2 * m + 1):
                v_copy(p, other_core[n], f_send.at[n], mate).wait_recv()
            if m < CHUNKS - 1:

                def tile(t, c, m=m):
                    at = pl.ds(pl.multiple_of(t * TILE, TILE), TILE)
                    if m == 0:
                        total[at, :] = product(m, at)
                    else:
                        total[at, :] += product(m, at)
                    return c

                lax.fori_loop(0, ROWS // TILE, tile, 0)

        def p_copy(n):
            return pltpu.make_async_remote_copy(
                src_ref=partial.at[cols[n]],
                dst_ref=arrived.at[p, col],
                send_sem=p_send.at[n],
                recv_sem=p_recv.at[p, col],
                device_id=(row, cols[n]),
                device_id_type=MESH,
            )

        def p_exchange(n, act):
            if n >= 2:
                act(p_copy(n))
            else:

                @pl.when(zl != n)
                def _():
                    act(p_copy(n))

        for j in (1, 3, 2, 0):
            xx = (x + j) % 4
            at = pl.ds(pl.multiple_of(xx * TILE, TILE), TILE)
            value = (total[at, :] + product(CHUNKS - 1, at)).astype(jnp.bfloat16)
            partial[pl.ds(xx * 2, 2)] = value.reshape(2, OWN, VECTORS)
            for n in (2 * j, 2 * j + 1):
                p_exchange(n, lambda c: c.start())

        for m in range(7):
            v_copy(p, row, g_send.at[m + 1], same_core[m + 1]).wait_send()
            v_copy(p, same_core[m + 1], f_send.at[m + 1], mate).wait_send()
        v_copy(p, row, g_send.at[0], mate).wait_send()

        arrived[p, col] = partial[col]
        for j in range(1, N_COL):
            s = (col + j) % N_COL
            pltpu.make_async_remote_copy(
                src_ref=partial.at[s],
                dst_ref=arrived.at[p, s],
                send_sem=p_send.at[0],
                recv_sem=p_recv.at[p, s],
                device_id=(row, s),
                device_id_type=MESH,
            ).wait_recv()
        for n in range(N_COL):
            p_exchange(n, lambda c: c.wait_send())

        applied = arrived[p, 0].astype(jnp.float32)
        for s in range(1, N_COL):
            applied = applied + arrived[p, s].astype(jnp.float32)
        now = current[...]
        scale = jnp.where(k == 0, 1.0, 2.0)
        following = scale * (applied - center * now) / half - previous[...]
        previous[...] = now
        current[...] = following
        gathered[1 - p, row // 4, pl.ds(pl.multiple_of((row % 4) * OWN, OWN), OWN), :] = (
            following.astype(jnp.bfloat16)
        )
        return carry

    lax.fori_loop(0, DEGREE, step, 0)
    out_ref[...] = current[...]


def body(trial_vectors, h_blocks, block_col, block_count, center, half_width):
    slot = lax.broadcasted_iota(jnp.int32, (DOMAIN, N_ROW, PER), 2)
    filled = slot < block_count[0, 0][:, :, None]
    code = jnp.where(filled, block_col[0, 0], -1)
    coef = (code[..., None] == jnp.arange(BLOCK_ROWS, dtype=jnp.int32)).astype(jnp.float32)
    scal = jnp.concatenate([center, half_width])
    vmem, smem = (
        pl.BlockSpec(memory_space=pltpu.VMEM),
        pl.BlockSpec(memory_space=pltpu.SMEM),
    )
    dma = pltpu.SemaphoreType.DMA
    bf16, f32 = jnp.bfloat16, jnp.float32
    return pl.pallas_call(
        kernel,
        out_shape=jax.ShapeDtypeStruct((OWN, VECTORS), f32),
        in_specs=[smem, smem, vmem, pl.BlockSpec(memory_space=pl.ANY)],
        out_specs=vmem,
        scratch_shapes=[
            pltpu.VMEM((N_ROW, DOMAIN, BLOCK, PER * BLOCK), bf16),
            pltpu.VMEM((CHUNKS, ROWS, CHUNK), bf16),
            pltpu.VMEM((2, CHUNKS, CHUNK, VECTORS), bf16),
            pltpu.VMEM((ROWS, VECTORS), f32),
            pltpu.VMEM((N_COL, OWN, VECTORS), bf16),
            pltpu.VMEM((2, N_COL, OWN, VECTORS), bf16),
            pltpu.VMEM((OWN, VECTORS), f32),
            pltpu.VMEM((OWN, VECTORS), f32),
            dma((N_ROW,)),
            dma((N_ROW,)),
            dma,
            dma((8,)),
            dma((8,)),
            dma((2, N_ROW)),
            dma((N_COL,)),
            dma((2, N_COL)),
        ],
        compiler_params=pltpu.CompilerParams(
            collective_id=0, has_side_effects=True, vmem_limit_bytes=48 * 2**20
        ),
        name="filter",
    )(coef.reshape(-1), scal, trial_vectors, h_blocks[0, :, :, :, 0, :])


def solution(mesh):
    in_specs = (
        P(("row", "col"), None),
        P("col", None, None, None, "row", None),
        P("col", "row", None, None, None),
        P("col", "row", None, None),
        P(),
        P(),
    )
    out_specs = P(("row", "col"), None)
    return jax.shard_map(body, mesh=mesh, in_specs=in_specs, out_specs=out_specs, check_vma=False)
```

```python
import jax
import jax.numpy as jnp
from jax import lax
from jax.experimental import pallas as pl
from jax.experimental.pallas import tpu as pltpu
from jax.sharding import PartitionSpec as P

BLOCK = 64
VECTORS = 256
PER = 2
DEGREE = 6
BLOCK_ROWS = 3
N_ROW = 16
N_COL = 8
OWN = BLOCK_ROWS * BLOCK
DOMAIN = BLOCK_ROWS * N_COL
ROWS = DOMAIN * BLOCK
CHIPS = 8
CHUNKS = 4
CHUNK = 4 * OWN
PIECES = 8
PIECE = DOMAIN // PIECES
MESH = pl.DeviceIdType.MESH
GATHER_ORDER = (1, 3, 2, 4, 5, 7, 6)
H_ORDER = (
    (1, 0, 0), (0, 1, 0), (0, 3, 0), (1, 0, 1), (0, 1, 1), (0, 3, 1), (1, 2, 0), (0, 2, 0),
    (1, 2, 1), (0, 2, 1), (1, 1, 0), (1, 3, 0), (1, 1, 1), (1, 3, 1), (0, 0, 1),
)
SCATTER_ORDER = ((2, 1), (3, 1), (2, 0), (3, 0), (1, 1), (0, 1), (1, 0))
SCATTER_READY = ((0, 1, 2, 3), (4, 5, 6))


def flip(value):
    return value + 1 - 2 * (value % 2)


def kernel(
    coef_ref,
    scal_ref,
    trial_ref,
    h_ref,
    out_ref,
    hbuf,
    dense,
    gathered,
    total,
    partial,
    arrived,
    current,
    previous,
    h_send,
    h_recv,
    g_send,
    f_send,
    g_recv,
    p_send,
    p_recv,
):
    row, col = lax.axis_index("row"), lax.axis_index("col")
    core, y, zh = row % 2, (row // 2) % 4, row // 8
    x, zl = col // 2, col % 2
    mate = flip(row)

    def chip(dz, dy, dc=0):
        return ((zh + dz) % 2) * 8 + ((y + dy) % 4) * 2 + (core + dc) % 2

    def pair_y(j):
        base = y if j < 2 else (y + 2) % 4
        return flip(base) if j % 2 else base

    same_core = [
        (zh if m < 4 else 1 - zh) * 8 + pair_y(m % 4) * 2 + core for m in range(CHIPS)
    ]

    barrier = pltpu.get_barrier_semaphore()
    for step_to in H_ORDER:
        pl.semaphore_signal(
            barrier, inc=1, device_id=(chip(*step_to), col), device_id_type=MESH
        )
    for j in range(1, N_COL):
        pl.semaphore_signal(
            barrier, inc=1, device_id=(row, (col + j) % N_COL), device_id_type=MESH
        )
    pl.semaphore_wait(barrier, N_ROW + N_COL - 2)

    def v_slot(p, s):
        return gathered.at[p, s // 4, pl.ds(pl.multiple_of((s % 4) * OWN, OWN), OWN), :]

    def v_copy(p, s, sem, to):
        return pltpu.make_async_remote_copy(
            src_ref=v_slot(p, s),
            dst_ref=v_slot(p, s),
            send_sem=sem,
            recv_sem=g_recv.at[p, s],
            device_id=(to, col),
            device_id_type=MESH,
        )

    def start_gather(p):
        v_copy(p, row, g_send.at[0], mate).start()
        for m in GATHER_ORDER:
            v_copy(p, row, g_send.at[m], same_core[m]).start()

    current[...] = trial_ref[...].astype(jnp.float32)
    previous[...] = jnp.zeros_like(previous)
    gathered[0, row // 4, pl.ds(pl.multiple_of((row % 4) * OWN, OWN), OWN), :] = trial_ref[...]
    start_gather(0)

    def h_copy(i, n, to):
        return pltpu.make_async_remote_copy(
            src_ref=h_ref.at[to, pl.ds(i * PIECE, PIECE)],
            dst_ref=hbuf.at[i, row],
            send_sem=h_send.at[i, n],
            recv_sem=h_recv.at[i],
            device_id=(to, col),
            device_id_type=MESH,
        )

    def h_own(i):
        return pltpu.make_async_copy(
            h_ref.at[row, pl.ds(i * PIECE, PIECE)], hbuf.at[i, row], h_recv.at[i]
        )

    def h_start(i, c):
        for n, step_to in enumerate(H_ORDER):
            h_copy(i, n, chip(*step_to)).start()
        h_own(i).start()
        return c

    lax.fori_loop(0, PIECES, h_start, 0)

    left = lax.broadcasted_iota(jnp.int32, (BLOCK, 2 * BLOCK), 1) < BLOCK

    def expand(piece, pair):
        even, odd = pair * 2, pair * 2 + 1

        def one(at_piece, carry):
            i = piece * PIECE + at_piece

            def coef(s, q, j):
                return coef_ref[((i * N_ROW + s) * PER + q) * BLOCK_ROWS + j]

            def lanes(a, b):
                return jnp.where(left, a, b)

            be = hbuf[piece, even, at_piece].astype(jnp.float32)
            bo = hbuf[piece, odd, at_piece].astype(jnp.float32)
            re, ro = pltpu.roll(be, BLOCK, 1), pltpu.roll(bo, BLOCK, 1)
            first = be * lanes(coef(even, 0, 0), coef(even, 1, 1)) + re * lanes(
                coef(even, 1, 0), coef(even, 0, 1)
            )
            middle = jnp.where(
                left,
                be * coef(even, 0, 2) + re * coef(even, 1, 2),
                bo * coef(odd, 1, 0) + ro * coef(odd, 0, 0),
            )
            last = bo * lanes(coef(odd, 0, 1), coef(odd, 1, 2)) + ro * lanes(
                coef(odd, 1, 1), coef(odd, 0, 2)
            )
            at = pl.ds(pl.multiple_of(i * BLOCK, BLOCK), BLOCK)
            offset = (pair % 2) * (2 * OWN)
            for k, part in enumerate((first, middle, last)):
                dense[
                    pair // 2,
                    at,
                    pl.ds(pl.multiple_of(offset + k * 2 * BLOCK, 2 * BLOCK), 2 * BLOCK),
                ] = part.astype(jnp.bfloat16)
            return carry

        lax.fori_loop(0, PIECE, one, 0)

    def h_arrive(i, c):
        pltpu.make_async_copy(hbuf.at[i], hbuf.at[i], h_recv.at[i]).wait()

        def one_pair(pair, cc):
            expand(i, pair)
            return cc

        lax.fori_loop(0, N_ROW // 2, one_pair, 0)
        return c

    lax.fori_loop(0, PIECES, h_arrive, 0)

    def h_sent(i, c):
        for n, step_to in enumerate(H_ORDER):
            h_copy(i, n, chip(*step_to)).wait_send()
        return c

    lax.fori_loop(0, PIECES, h_sent, 0)

    center, half = scal_ref[0], scal_ref[1]
    HALF = ROWS // 2

    def step(k, carry):
        p = k % 2

        @pl.when(k > 0)
        def _():
            start_gather(p)

        def product(chunk, rows_at):
            return jnp.dot(
                dense[chunk, rows_at, :],
                gathered[p, chunk],
                preferred_element_type=jnp.float32,
            )

        here = {0}
        done = 0
        for m in GATHER_ORDER:
            v_copy(p, same_core[m], f_send.at[m], mate).wait_recv()
            v_copy(p, same_core[m], f_send.at[m], mate).start()
            here.add(m)
            if m ^ 1 in here:
                for n in (m, m ^ 1):
                    v_copy(p, flip(same_core[n]), f_send.at[n], mate).wait_recv()
                chunk = same_core[m] // 4
                done += 1
                if done == 1:
                    total[...] = product(chunk, slice(None))
                elif done < CHUNKS:
                    total[...] += product(chunk, slice(None))

        def p_copy(n):
            j, dl = SCATTER_ORDER[n]
            base = x if j < 2 else (x + 2) % 4
            to = (flip(base) if j % 2 else base) * 2 + (zl + dl) % 2
            return pltpu.make_async_remote_copy(
                src_ref=partial.at[to],
                dst_ref=arrived.at[p, col],
                send_sem=p_send.at[n],
                recv_sem=p_recv.at[p, col],
                device_id=(row, to),
                device_id_type=MESH,
            )

        for half_at, ready in enumerate(SCATTER_READY):
            first = (x // 2 + 1 + half_at) % 2
            at = pl.ds(pl.multiple_of(first * HALF, HALF), HALF)
            value = (total[at, :] + product(chunk, at)).astype(jnp.bfloat16)
            partial[pl.ds(first * 4, 4)] = value.reshape(4, OWN, VECTORS)
            for n in ready:
                p_copy(n).start()

        v_copy(p, row, g_send.at[0], mate).wait_send()
        for m in range(1, CHIPS):
            v_copy(p, row, g_send.at[m], mate).wait_send()
            v_copy(p, same_core[m], f_send.at[m], mate).wait_send()

        arrived[p, col] = partial[col]
        for j in range(1, N_COL):
            s = (col + j) % N_COL
            pltpu.make_async_remote_copy(
                src_ref=partial.at[s],
                dst_ref=arrived.at[p, s],
                send_sem=p_send.at[0],
                recv_sem=p_recv.at[p, s],
                device_id=(row, s),
                device_id_type=MESH,
            ).wait_recv()
        for n in range(N_COL - 1):
            p_copy(n).wait_send()

        applied = arrived[p, 0].astype(jnp.float32)
        for s in range(1, N_COL):
            applied = applied + arrived[p, s].astype(jnp.float32)
        now = current[...]
        scale = jnp.where(k == 0, 1.0, 2.0)
        following = scale * (applied - center * now) / half - previous[...]
        previous[...] = now
        current[...] = following
        gathered[1 - p, row // 4, pl.ds(pl.multiple_of((row % 4) * OWN, OWN), OWN), :] = (
            following.astype(jnp.bfloat16)
        )
        return carry

    lax.fori_loop(0, DEGREE, step, 0)
    out_ref[...] = current[...]


def body(trial_vectors, h_blocks, block_col, block_count, center, half_width):
    slot = lax.broadcasted_iota(jnp.int32, (DOMAIN, N_ROW, PER), 2)
    filled = slot < block_count[0, 0][:, :, None]
    code = jnp.where(filled, block_col[0, 0], -1)
    coef = (code[..., None] == jnp.arange(BLOCK_ROWS, dtype=jnp.int32)).astype(jnp.float32)
    scal = jnp.concatenate([center, half_width])
    vmem, smem = (
        pl.BlockSpec(memory_space=pltpu.VMEM),
        pl.BlockSpec(memory_space=pltpu.SMEM),
    )
    dma = pltpu.SemaphoreType.DMA
    bf16, f32 = jnp.bfloat16, jnp.float32
    return pl.pallas_call(
        kernel,
        out_shape=jax.ShapeDtypeStruct((OWN, VECTORS), f32),
        in_specs=[smem, smem, vmem, pl.BlockSpec(memory_space=pl.ANY)],
        out_specs=vmem,
        scratch_shapes=[
            pltpu.VMEM((PIECES, N_ROW, PIECE, BLOCK, PER * BLOCK), bf16),
            pltpu.VMEM((CHUNKS, ROWS, CHUNK), bf16),
            pltpu.VMEM((2, CHUNKS, CHUNK, VECTORS), bf16),
            pltpu.VMEM((ROWS, VECTORS), f32),
            pltpu.VMEM((N_COL, OWN, VECTORS), bf16),
            pltpu.VMEM((2, N_COL, OWN, VECTORS), bf16),
            pltpu.VMEM((OWN, VECTORS), f32),
            pltpu.VMEM((OWN, VECTORS), f32),
            dma((PIECES, N_ROW - 1)),
            dma((PIECES,)),
            dma((CHIPS,)),
            dma((CHIPS,)),
            dma((2, N_ROW)),
            dma((N_COL - 1,)),
            dma((2, N_COL)),
        ],
        compiler_params=pltpu.CompilerParams(
            collective_id=0, has_side_effects=True, vmem_limit_bytes=48 * 2**20
        ),
        name="filter",
    )(coef.reshape(-1), scal, trial_vectors, h_blocks[0, :, :, :, 0, :])


def solution(mesh):
    in_specs = (
        P(("row", "col"), None),
        P("col", None, None, None, "row", None),
        P("col", "row", None, None, None),
        P("col", "row", None, None),
        P(),
        P(),
    )
    out_specs = P(("row", "col"), None)
    return jax.shard_map(body, mesh=mesh, in_specs=in_specs, out_specs=out_specs, check_vma=False)
```

```python
import jax
import jax.numpy as jnp
from jax import lax
from jax.experimental import pallas as pl
from jax.experimental.pallas import tpu as pltpu
from jax.sharding import PartitionSpec as P

BLOCK = 64
VECTORS = 256
PER = 2
DEGREE = 6
BLOCK_ROWS = 3
N_ROW = 16
N_COL = 8
WIDTH = VECTORS // 2
TURNS = 2 * DEGREE
OWN = BLOCK_ROWS * BLOCK
DOMAIN = BLOCK_ROWS * N_COL
ROWS = DOMAIN * BLOCK
CHIPS = 8
CHUNK = 8 * OWN
PIECES = 8
PIECE = DOMAIN // PIECES
MESH = pl.DeviceIdType.MESH
GATHER_ORDER = (4, 1, 3, 2)
RELAY_ORDER = (1, 3, 2)
ARRIVAL_ORDER = (4, 1, 3, 2, 5, 7, 6)
FINISH_AT = 4
H_ORDER = (
    (1, 0, 0), (0, 1, 0), (0, 3, 0), (1, 0, 1), (0, 1, 1), (0, 3, 1), (1, 2, 0), (0, 2, 0),
    (1, 2, 1), (0, 2, 1), (1, 1, 0), (1, 3, 0), (1, 1, 1), (1, 3, 1), (0, 0, 1),
)
SCATTER_ORDER = ((2, 1), (3, 1), (2, 0), (3, 0), (1, 1), (0, 1), (1, 0))
SCATTER_READY = ((0, 1, 2, 3), (4, 5, 6))


def flip(value):
    return value + 1 - 2 * (value % 2)


def kernel(
    coef_ref,
    scal_ref,
    trial_ref,
    h_ref,
    out_ref,
    hbuf,
    dense,
    gathered,
    total,
    partial,
    arrived,
    current,
    previous,
    h_send,
    h_recv,
    g_send,
    r_send,
    f_send,
    f_recv,
    g_recv,
    p_send,
    p_recv,
):
    row, col = lax.axis_index("row"), lax.axis_index("col")
    core, y, zh = row % 2, (row // 2) % 4, row // 8
    x, zl = col // 2, col % 2
    mate = flip(row)

    def chip(dz, dy, dc=0):
        return ((zh + dz) % 2) * 8 + ((y + dy) % 4) * 2 + (core + dc) % 2

    def pair_y(j):
        base = y if j < 2 else (y + 2) % 4
        return flip(base) if j % 2 else base

    same_core = [
        (zh if m < 4 else 1 - zh) * 8 + pair_y(m % 4) * 2 + core for m in range(CHIPS)
    ]

    barrier = pltpu.get_barrier_semaphore()
    for step_to in H_ORDER:
        pl.semaphore_signal(
            barrier, inc=1, device_id=(chip(*step_to), col), device_id_type=MESH
        )
    for j in range(1, N_COL):
        pl.semaphore_signal(
            barrier, inc=1, device_id=(row, (col + j) % N_COL), device_id_type=MESH
        )
    pl.semaphore_wait(barrier, N_ROW + N_COL - 2)

    def v_rows(s):
        place = (s % 2) * 4 + (s // 2) % 4
        return pl.ds(pl.multiple_of(place * OWN, OWN), OWN)

    def v_slot(b, s):
        return gathered.at[b, s // 8, v_rows(s), :]

    def v_copy(b, s, sem, to):
        return pltpu.make_async_remote_copy(
            src_ref=v_slot(b, s),
            dst_ref=v_slot(b, s),
            send_sem=sem,
            recv_sem=g_recv.at[b, s // 2],
            device_id=(to, col),
            device_id_type=MESH,
        )

    def share(b, m):
        s = same_core[m]
        return pltpu.make_async_remote_copy(
            src_ref=v_slot(b, s),
            dst_ref=v_slot(b, s),
            send_sem=f_send.at[b % 2, m],
            recv_sem=f_recv.at[b, s // 8],
            device_id=(mate, col),
            device_id_type=MESH,
        )

    def shared(b, z):
        half_slot = gathered.at[b, z, pl.ds(pl.multiple_of((1 - core) * 4 * OWN, OWN), 4 * OWN), :]
        pltpu.make_async_copy(half_slot, half_slot, f_recv.at[b, z]).wait()

    def start_gather(t, value):
        b, h = t % 4, t % 2
        gathered[b, zh, v_rows(row), :] = value
        for m in GATHER_ORDER:
            v_copy(b, row, g_send.at[h, m], same_core[m]).start()
        share(b, 0).start()

    def relay(b, m):
        return v_copy(b, same_core[4], r_send.at[m], same_core[m])

    for h in range(2):
        value = trial_ref[:, h * WIDTH : (h + 1) * WIDTH]
        current[h] = value.astype(jnp.float32)
        start_gather(h, value)
    previous[...] = jnp.zeros_like(previous)

    def h_copy(i, n, to):
        return pltpu.make_async_remote_copy(
            src_ref=h_ref.at[to, pl.ds(i * PIECE, PIECE)],
            dst_ref=hbuf.at[i, row],
            send_sem=h_send.at[i, n],
            recv_sem=h_recv.at[i],
            device_id=(to, col),
            device_id_type=MESH,
        )

    def h_own(i):
        return pltpu.make_async_copy(
            h_ref.at[row, pl.ds(i * PIECE, PIECE)], hbuf.at[i, row], h_recv.at[i]
        )

    def h_start(i, c):
        for n, step_to in enumerate(H_ORDER):
            h_copy(i, n, chip(*step_to)).start()
        h_own(i).start()
        return c

    lax.fori_loop(0, PIECES, h_start, 0)

    left = lax.broadcasted_iota(jnp.int32, (BLOCK, 2 * BLOCK), 1) < BLOCK

    def expand(piece, pair):
        even = (pair // 4) * 8 + (pair % 2) * 4 + (pair // 2) % 2
        odd = even + 2

        def one(at_piece, carry):
            i = piece * PIECE + at_piece

            def coef(s, q, j):
                return coef_ref[((i * N_ROW + s) * PER + q) * BLOCK_ROWS + j]

            def lanes(a, b):
                return jnp.where(left, a, b)

            be = hbuf[piece, even, at_piece].astype(jnp.float32)
            bo = hbuf[piece, odd, at_piece].astype(jnp.float32)
            re, ro = pltpu.roll(be, BLOCK, 1), pltpu.roll(bo, BLOCK, 1)
            first = be * lanes(coef(even, 0, 0), coef(even, 1, 1)) + re * lanes(
                coef(even, 1, 0), coef(even, 0, 1)
            )
            middle = jnp.where(
                left,
                be * coef(even, 0, 2) + re * coef(even, 1, 2),
                bo * coef(odd, 1, 0) + ro * coef(odd, 0, 0),
            )
            last = bo * lanes(coef(odd, 0, 1), coef(odd, 1, 2)) + ro * lanes(
                coef(odd, 1, 1), coef(odd, 0, 2)
            )
            at = pl.ds(pl.multiple_of(i * BLOCK, BLOCK), BLOCK)
            offset = (pair % 4) * (2 * OWN)
            for k, part in enumerate((first, middle, last)):
                dense[
                    pair // 4,
                    at,
                    pl.ds(pl.multiple_of(offset + k * 2 * BLOCK, 2 * BLOCK), 2 * BLOCK),
                ] = part.astype(jnp.bfloat16)
            return carry

        lax.fori_loop(0, PIECE, one, 0)

    def h_arrive(i, c):
        pltpu.make_async_copy(hbuf.at[i], hbuf.at[i], h_recv.at[i]).wait()

        def one_pair(pair, cc):
            expand(i, pair)
            return cc

        lax.fori_loop(0, N_ROW // 2, one_pair, 0)
        return c

    lax.fori_loop(0, PIECES, h_arrive, 0)

    def h_sent(i, c):
        for n, step_to in enumerate(H_ORDER):
            h_copy(i, n, chip(*step_to)).wait_send()
        return c

    lax.fori_loop(0, PIECES, h_sent, 0)

    center, half = scal_ref[0], scal_ref[1]
    HALF = ROWS // 2

    def p_copy(t, n):
        j, dl = SCATTER_ORDER[n]
        base = x if j < 2 else (x + 2) % 4
        to = (flip(base) if j % 2 else base) * 2 + (zl + dl) % 2
        return pltpu.make_async_remote_copy(
            src_ref=partial.at[t % 2, to],
            dst_ref=arrived.at[t % 4, col],
            send_sem=p_send.at[t % 2, n],
            recv_sem=p_recv.at[t % 4, col],
            device_id=(row, to),
            device_id_type=MESH,
        )

    def multiply(t, finish_other):
        b, h = t % 4, t % 2

        def product(chunk, rows_at):
            return jnp.dot(
                dense[chunk, rows_at, :],
                gathered[b, chunk],
                preferred_element_type=jnp.float32,
            )

        def arrive(m):
            v_copy(b, same_core[m], g_send.at[h, 1], mate).wait_recv()
            if m == 4:
                for n in RELAY_ORDER:
                    relay(b, n).start()
            share(b, m).start()

        for m in ARRIVAL_ORDER[:FINISH_AT]:
            arrive(m)
        shared(b, zh)
        total[...] = product(zh, slice(None))
        finish_other()
        for m in ARRIVAL_ORDER[FINISH_AT:]:
            arrive(m)
        shared(b, 1 - zh)

        for half_at, ready in enumerate(SCATTER_READY):
            first = (x // 2 + 1 + half_at) % 2
            at = pl.ds(pl.multiple_of(first * HALF, HALF), HALF)
            value = (total[at, :] + product(1 - zh, at)).astype(jnp.bfloat16)
            partial[h, pl.ds(first * 4, 4)] = value.reshape(4, OWN, WIDTH)
            for n in ready:
                p_copy(t, n).start()

        for m in GATHER_ORDER:
            v_copy(b, row, g_send.at[h, m], mate).wait_send()
        for m in RELAY_ORDER:
            relay(b, m).wait_send()
        for m in range(CHIPS):
            share(b, m).wait_send()

    def finish(t):
        b, h = t % 4, t % 2
        arrived[b, col] = partial[h, col]
        for j in range(1, N_COL):
            s = (col + j) % N_COL
            pltpu.make_async_remote_copy(
                src_ref=partial.at[h, s],
                dst_ref=arrived.at[b, s],
                send_sem=p_send.at[h, 0],
                recv_sem=p_recv.at[b, s],
                device_id=(row, s),
                device_id_type=MESH,
            ).wait_recv()
        for n in range(N_COL - 1):
            p_copy(t, n).wait_send()

        applied = arrived[b, 0].astype(jnp.float32)
        for s in range(1, N_COL):
            applied = applied + arrived[b, s].astype(jnp.float32)
        now = current[h]
        scale = jnp.where(t < 2, 1.0, 2.0)
        following = scale * (applied - center * now) / half - previous[h]
        previous[h] = now
        current[h] = following
        return following

    def turn(t, carry):
        def finish_other():
            @pl.when(t > 0)
            def _():
                following = finish(t - 1)

                @pl.when(t < TURNS - 1)
                def _():
                    start_gather(t + 1, following.astype(jnp.bfloat16))

        multiply(t, finish_other)
        return carry

    lax.fori_loop(0, TURNS, turn, 0)
    finish(TURNS - 1)
    for h in range(2):
        out_ref[:, h * WIDTH : (h + 1) * WIDTH] = current[h]


def body(trial_vectors, h_blocks, block_col, block_count, center, half_width):
    slot = lax.broadcasted_iota(jnp.int32, (DOMAIN, N_ROW, PER), 2)
    filled = slot < block_count[0, 0][:, :, None]
    code = jnp.where(filled, block_col[0, 0], -1)
    coef = (code[..., None] == jnp.arange(BLOCK_ROWS, dtype=jnp.int32)).astype(jnp.float32)
    scal = jnp.concatenate([center, half_width])
    vmem, smem = (
        pl.BlockSpec(memory_space=pltpu.VMEM),
        pl.BlockSpec(memory_space=pltpu.SMEM),
    )
    dma = pltpu.SemaphoreType.DMA
    bf16, f32 = jnp.bfloat16, jnp.float32
    return pl.pallas_call(
        kernel,
        out_shape=jax.ShapeDtypeStruct((OWN, VECTORS), f32),
        in_specs=[smem, smem, vmem, pl.BlockSpec(memory_space=pl.ANY)],
        out_specs=vmem,
        scratch_shapes=[
            pltpu.VMEM((PIECES, N_ROW, PIECE, BLOCK, PER * BLOCK), bf16),
            pltpu.VMEM((2, ROWS, CHUNK), bf16),
            pltpu.VMEM((4, 2, CHUNK, WIDTH), bf16),
            pltpu.VMEM((ROWS, WIDTH), f32),
            pltpu.VMEM((2, N_COL, OWN, WIDTH), bf16),
            pltpu.VMEM((4, N_COL, OWN, WIDTH), bf16),
            pltpu.VMEM((2, OWN, WIDTH), f32),
            pltpu.VMEM((2, OWN, WIDTH), f32),
            dma((PIECES, N_ROW - 1)),
            dma((PIECES,)),
            dma((2, 5)),
            dma((4,)),
            dma((2, CHIPS)),
            dma((4, 2)),
            dma((4, CHIPS)),
            dma((2, N_COL - 1)),
            dma((4, N_COL)),
        ],
        compiler_params=pltpu.CompilerParams(
            collective_id=0, has_side_effects=True, vmem_limit_bytes=48 * 2**20
        ),
        name="filter",
    )(coef.reshape(-1), scal, trial_vectors, h_blocks[0, :, :, :, 0, :])


def solution(mesh):
    in_specs = (
        P(("row", "col"), None),
        P("col", None, None, None, "row", None),
        P("col", "row", None, None, None),
        P("col", "row", None, None),
        P(),
        P(),
    )
    out_specs = P(("row", "col"), None)
    return jax.shard_map(body, mesh=mesh, in_specs=in_specs, out_specs=out_specs, check_vma=False)
```

```python
import jax
import jax.numpy as jnp
from jax import lax
from jax.experimental import pallas as pl
from jax.experimental.pallas import tpu as pltpu
from jax.sharding import PartitionSpec as P

BLOCK = 64
VECTORS = 256
PER = 2
DEGREE = 6
BLOCK_ROWS = 3
N_ROW = 16
N_COL = 8
WIDTH = VECTORS // 2
TURNS = 2 * DEGREE
OWN = BLOCK_ROWS * BLOCK
DOMAIN = BLOCK_ROWS * N_COL
ROWS = DOMAIN * BLOCK
CHIPS = 8
CHUNK = 8 * OWN
PIECES = 12
PIECE = DOMAIN // PIECES
MESH = pl.DeviceIdType.MESH
GATHER_ORDER = (4, 1, 3, 2)
RELAY_ORDER = (1, 3, 2)
ARRIVAL_ORDER = (4, 1, 3, 2, 5, 7, 6)
FINISH_AT = 4
H_ORDER = (
    (1, 0, 0), (0, 1, 0), (0, 3, 0), (1, 0, 1), (0, 1, 1), (0, 3, 1), (1, 2, 0), (0, 2, 0),
    (1, 2, 1), (0, 2, 1), (1, 1, 0), (1, 3, 0), (1, 1, 1), (1, 3, 1), (0, 0, 1),
)
SCATTER_ORDER = ((2, 1), (3, 1), (2, 0), (3, 0), (1, 1), (0, 1), (1, 0))
SCATTER_READY = ((0, 1, 2, 3), (4, 5, 6))


def flip(value):
    return value + 1 - 2 * (value % 2)


def kernel(
    code_ref,
    center_ref,
    half_ref,
    trial_in,
    h_ref,
    out_ref,
    trial_ref,
    trial_sem,
    hbuf,
    dense,
    gathered,
    total,
    partial,
    arrived,
    current,
    previous,
    h_send,
    h_recv,
    g_send,
    r_send,
    f_send,
    f_recv,
    g_recv,
    p_send,
    p_recv,
):
    row, col = lax.axis_index("row"), lax.axis_index("col")
    core, y, zh = row % 2, (row // 2) % 4, row // 8
    x, zl = col // 2, col % 2
    mate = flip(row)

    def chip(dz, dy, dc=0):
        return ((zh + dz) % 2) * 8 + ((y + dy) % 4) * 2 + (core + dc) % 2

    def pair_y(j):
        base = y if j < 2 else (y + 2) % 4
        return flip(base) if j % 2 else base

    same_core = [
        (zh if m < 4 else 1 - zh) * 8 + pair_y(m % 4) * 2 + core for m in range(CHIPS)
    ]

    trial_copy = pltpu.make_async_copy(trial_in, trial_ref, trial_sem)
    trial_copy.start()
    barrier = pltpu.get_barrier_semaphore()
    for step_to in H_ORDER:
        pl.semaphore_signal(
            barrier, inc=1, device_id=(chip(*step_to), col), device_id_type=MESH
        )
    for j in range(1, N_COL):
        pl.semaphore_signal(
            barrier, inc=1, device_id=(row, (col + j) % N_COL), device_id_type=MESH
        )
    pl.semaphore_wait(barrier, N_ROW + N_COL - 2)
    trial_copy.wait()

    def v_rows(s):
        place = (s % 2) * 4 + (s // 2) % 4
        return pl.ds(pl.multiple_of(place * OWN, OWN), OWN)

    def v_slot(b, s):
        return gathered.at[b, s // 8, v_rows(s), :]

    def v_copy(b, s, sem, to):
        return pltpu.make_async_remote_copy(
            src_ref=v_slot(b, s),
            dst_ref=v_slot(b, s),
            send_sem=sem,
            recv_sem=g_recv.at[b, s // 2],
            device_id=(to, col),
            device_id_type=MESH,
        )

    def share(b, m):
        s = same_core[m]
        return pltpu.make_async_remote_copy(
            src_ref=v_slot(b, s),
            dst_ref=v_slot(b, s),
            send_sem=f_send.at[b % 2, m],
            recv_sem=f_recv.at[b, s // 8],
            device_id=(mate, col),
            device_id_type=MESH,
        )

    def shared(b, z):
        half_slot = gathered.at[b, z, pl.ds(pl.multiple_of((1 - core) * 4 * OWN, OWN), 4 * OWN), :]
        pltpu.make_async_copy(half_slot, half_slot, f_recv.at[b, z]).wait()

    def start_gather(t, value):
        b, h = t % 4, t % 2
        gathered[b, zh, v_rows(row), :] = value
        for m in GATHER_ORDER:
            v_copy(b, row, g_send.at[h, m], same_core[m]).start()
        share(b, 0).start()

    def relay(b, m):
        return v_copy(b, same_core[4], r_send.at[m], same_core[m])

    for h in range(2):
        value = trial_ref[:, h * WIDTH : (h + 1) * WIDTH]
        current[h] = value.astype(jnp.float32)
        start_gather(h, value)
    previous[...] = jnp.zeros_like(previous)

    def h_copy(i, n, to):
        return pltpu.make_async_remote_copy(
            src_ref=h_ref.at[to, pl.ds(i * PIECE, PIECE)],
            dst_ref=hbuf.at[i, row],
            send_sem=h_send.at[i, n],
            recv_sem=h_recv.at[i],
            device_id=(to, col),
            device_id_type=MESH,
        )

    def h_own(i):
        return pltpu.make_async_copy(
            h_ref.at[row, pl.ds(i * PIECE, PIECE)], hbuf.at[i, row], h_recv.at[i]
        )

    def h_start(i, c):
        for n, step_to in enumerate(H_ORDER):
            h_copy(i, n, chip(*step_to)).start()
        h_own(i).start()
        return c

    lax.fori_loop(0, PIECES, h_start, 0)

    left = lax.broadcasted_iota(jnp.int32, (BLOCK, 2 * BLOCK), 1) < BLOCK

    def expand(piece, pair):
        even = (pair // 4) * 8 + (pair % 2) * 4 + (pair // 2) % 2
        odd = even + 2

        def one(at_piece, carry):
            i = piece * PIECE + at_piece

            def coef(s, q, j):
                return jnp.where(code_ref[(i * N_ROW + s) * PER + q] == j, 1.0, 0.0)

            def lanes(a, b):
                return jnp.where(left, a, b)

            be = hbuf[piece, even, at_piece].astype(jnp.float32)
            bo = hbuf[piece, odd, at_piece].astype(jnp.float32)
            re, ro = pltpu.roll(be, BLOCK, 1), pltpu.roll(bo, BLOCK, 1)
            first = be * lanes(coef(even, 0, 0), coef(even, 1, 1)) + re * lanes(
                coef(even, 1, 0), coef(even, 0, 1)
            )
            middle = jnp.where(
                left,
                be * coef(even, 0, 2) + re * coef(even, 1, 2),
                bo * coef(odd, 1, 0) + ro * coef(odd, 0, 0),
            )
            last = bo * lanes(coef(odd, 0, 1), coef(odd, 1, 2)) + ro * lanes(
                coef(odd, 1, 1), coef(odd, 0, 2)
            )
            at = pl.ds(pl.multiple_of(i * BLOCK, BLOCK), BLOCK)
            offset = (pair % 4) * (2 * OWN)
            for k, part in enumerate((first, middle, last)):
                dense[
                    pair // 4,
                    at,
                    pl.ds(pl.multiple_of(offset + k * 2 * BLOCK, 2 * BLOCK), 2 * BLOCK),
                ] = part.astype(jnp.bfloat16)
            return carry

        lax.fori_loop(0, PIECE, one, 0)

    def h_arrive(i, c):
        pltpu.make_async_copy(hbuf.at[i], hbuf.at[i], h_recv.at[i]).wait()

        def one_pair(pair, cc):
            expand(i, pair)
            return cc

        lax.fori_loop(0, N_ROW // 2, one_pair, 0)
        return c

    lax.fori_loop(0, PIECES, h_arrive, 0)

    def h_sent(i, c):
        for n, step_to in enumerate(H_ORDER):
            h_copy(i, n, chip(*step_to)).wait_send()
        return c

    lax.fori_loop(0, PIECES, h_sent, 0)

    center, half = center_ref[0], half_ref[0]
    HALF = ROWS // 2

    def p_copy(t, n):
        j, dl = SCATTER_ORDER[n]
        base = x if j < 2 else (x + 2) % 4
        to = (flip(base) if j % 2 else base) * 2 + (zl + dl) % 2
        return pltpu.make_async_remote_copy(
            src_ref=partial.at[t % 2, to],
            dst_ref=arrived.at[t % 4, col],
            send_sem=p_send.at[t % 2, n],
            recv_sem=p_recv.at[t % 4, col],
            device_id=(row, to),
            device_id_type=MESH,
        )

    def multiply(t, finish_other):
        b, h = t % 4, t % 2

        def product(chunk, rows_at):
            return jnp.dot(
                dense[chunk, rows_at, :],
                gathered[b, chunk],
                preferred_element_type=jnp.float32,
            )

        def arrive(m):
            v_copy(b, same_core[m], g_send.at[h, 1], mate).wait_recv()
            if m == 4:
                for n in RELAY_ORDER:
                    relay(b, n).start()
            share(b, m).start()

        for m in ARRIVAL_ORDER[:FINISH_AT]:
            arrive(m)
        shared(b, zh)
        total[...] = product(zh, slice(None))
        finish_other()
        for m in ARRIVAL_ORDER[FINISH_AT:]:
            arrive(m)
        shared(b, 1 - zh)

        for half_at, ready in enumerate(SCATTER_READY):
            first = (x // 2 + 1 + half_at) % 2
            at = pl.ds(pl.multiple_of(first * HALF, HALF), HALF)
            value = (total[at, :] + product(1 - zh, at)).astype(jnp.bfloat16)
            partial[h, pl.ds(first * 4, 4)] = value.reshape(4, OWN, WIDTH)
            for n in ready:
                p_copy(t, n).start()

        for m in GATHER_ORDER:
            v_copy(b, row, g_send.at[h, m], mate).wait_send()
        for m in RELAY_ORDER:
            relay(b, m).wait_send()
        for m in range(CHIPS):
            share(b, m).wait_send()

    def finish(t):
        b, h = t % 4, t % 2
        arrived[b, col] = partial[h, col]
        for j in range(1, N_COL):
            s = (col + j) % N_COL
            pltpu.make_async_remote_copy(
                src_ref=partial.at[h, s],
                dst_ref=arrived.at[b, s],
                send_sem=p_send.at[h, 0],
                recv_sem=p_recv.at[b, s],
                device_id=(row, s),
                device_id_type=MESH,
            ).wait_recv()
        for n in range(N_COL - 1):
            p_copy(t, n).wait_send()

        applied = arrived[b, 0].astype(jnp.float32)
        for s in range(1, N_COL):
            applied = applied + arrived[b, s].astype(jnp.float32)
        now = current[h]
        scale = jnp.where(t < 2, 1.0, 2.0)
        following = scale * (applied - center * now) / half - previous[h]
        previous[h] = now
        current[h] = following
        return following

    def turn(t, carry):
        def finish_other():
            @pl.when(t > 0)
            def _():
                following = finish(t - 1)

                @pl.when(t < TURNS - 1)
                def _():
                    start_gather(t + 1, following.astype(jnp.bfloat16))

        multiply(t, finish_other)
        return carry

    lax.fori_loop(0, TURNS, turn, 0)
    finish(TURNS - 1)
    for h in range(2):
        out_ref[:, h * WIDTH : (h + 1) * WIDTH] = current[h]


def body(trial_vectors, h_blocks, block_col, block_count, center, half_width):
    slot = lax.broadcasted_iota(jnp.int32, (DOMAIN, N_ROW, PER), 2)
    filled = slot < block_count[0, 0][:, :, None]
    code = jnp.where(filled, block_col[0, 0], -1)
    vmem, smem, hbm = (
        pl.BlockSpec(memory_space=space) for space in (pltpu.VMEM, pltpu.SMEM, pl.ANY)
    )
    dma = pltpu.SemaphoreType.DMA
    bf16, f32 = jnp.bfloat16, jnp.float32
    return pl.pallas_call(
        kernel,
        out_shape=jax.ShapeDtypeStruct((OWN, VECTORS), f32),
        in_specs=[smem, smem, smem, hbm, hbm],
        out_specs=vmem,
        scratch_shapes=[
            pltpu.VMEM((OWN, VECTORS), bf16),
            dma,
            pltpu.VMEM((PIECES, N_ROW, PIECE, BLOCK, PER * BLOCK), bf16),
            pltpu.VMEM((2, ROWS, CHUNK), bf16),
            pltpu.VMEM((4, 2, CHUNK, WIDTH), bf16),
            pltpu.VMEM((ROWS, WIDTH), f32),
            pltpu.VMEM((2, N_COL, OWN, WIDTH), bf16),
            pltpu.VMEM((4, N_COL, OWN, WIDTH), bf16),
            pltpu.VMEM((2, OWN, WIDTH), f32),
            pltpu.VMEM((2, OWN, WIDTH), f32),
            dma((PIECES, N_ROW - 1)),
            dma((PIECES,)),
            dma((2, 5)),
            dma((4,)),
            dma((2, CHIPS)),
            dma((4, 2)),
            dma((4, CHIPS)),
            dma((2, N_COL - 1)),
            dma((4, N_COL)),
        ],
        compiler_params=pltpu.CompilerParams(
            collective_id=0, has_side_effects=True, vmem_limit_bytes=48 * 2**20
        ),
        name="filter",
    )(code.reshape(-1), center, half_width, trial_vectors, h_blocks[0, :, :, :, 0, :])


def solution(mesh):
    in_specs = (
        P(("row", "col"), None),
        P("col", None, None, None, "row", None),
        P("col", "row", None, None, None),
        P("col", "row", None, None),
        P(),
        P(),
    )
    out_specs = P(("row", "col"), None)
    return jax.shard_map(body, mesh=mesh, in_specs=in_specs, out_specs=out_specs, check_vma=False)
```

```python
import jax
import jax.numpy as jnp
from jax import lax
from jax.experimental import pallas as pl
from jax.experimental.pallas import tpu as pltpu
from jax.sharding import PartitionSpec as P

BLOCK = 64
VECTORS = 256
PER = 2
DEGREE = 6
BLOCK_ROWS = 3
N_ROW = 16
N_COL = 8
WIDTH = VECTORS // 2
TURNS = 2 * DEGREE
OWN = BLOCK_ROWS * BLOCK
DOMAIN = BLOCK_ROWS * N_COL
ROWS = DOMAIN * BLOCK
CHIPS = 8
CHUNK = 8 * OWN
PIECES = 12
PIECE = DOMAIN // PIECES
MESH = pl.DeviceIdType.MESH
GATHER_ORDER = (4, 1, 3, 2)
RELAY_ORDER = (1, 3, 2)
ARRIVAL_ORDER = (4, 1, 3, 2, 5, 7, 6)
FINISH_AT = 4
H_ORDER = (
    (1, 0, 0), (0, 1, 0), (0, 3, 0), (1, 0, 1), (0, 1, 1), (0, 3, 1), (1, 2, 0), (0, 2, 0),
    (1, 2, 1), (0, 2, 1), (1, 1, 0), (1, 3, 0), (1, 1, 1), (1, 3, 1), (0, 0, 1),
)
SCATTER_ORDER = ((2, 1), (3, 1), (2, 0), (3, 0), (1, 1), (0, 1), (1, 0))
SCATTER_READY = ((0, 1, 2, 3), (4, 5, 6))


def flip(value):
    return value + 1 - 2 * (value % 2)


def kernel(
    code_ref,
    center_ref,
    half_ref,
    trial_in,
    h_ref,
    out_ref,
    trial_ref,
    trial_sem,
    hbuf,
    dense,
    gathered,
    total,
    partial,
    arrived,
    current,
    previous,
    h_send,
    h_recv,
    g_send,
    r_send,
    f_send,
    f_recv,
    g_recv,
    p_send,
    p_recv,
):
    row, col = lax.axis_index("row"), lax.axis_index("col")
    core, y, zh = row % 2, (row // 2) % 4, row // 8
    x, zl = col // 2, col % 2
    mate = flip(row)

    def chip(dz, dy, dc=0):
        return ((zh + dz) % 2) * 8 + ((y + dy) % 4) * 2 + (core + dc) % 2

    def pair_y(j):
        base = y if j < 2 else (y + 2) % 4
        return flip(base) if j % 2 else base

    same_core = [
        (zh if m < 4 else 1 - zh) * 8 + pair_y(m % 4) * 2 + core for m in range(CHIPS)
    ]

    trial_copy = pltpu.make_async_copy(trial_in, trial_ref, trial_sem)
    trial_copy.start()
    barrier = pltpu.get_barrier_semaphore()
    for step_to in H_ORDER:
        pl.semaphore_signal(
            barrier, inc=1, device_id=(chip(*step_to), col), device_id_type=MESH
        )
    for j in range(1, N_COL):
        pl.semaphore_signal(
            barrier, inc=1, device_id=(row, (col + j) % N_COL), device_id_type=MESH
        )
    pl.semaphore_wait(barrier, N_ROW + N_COL - 2)
    trial_copy.wait()

    def v_rows(s):
        place = (s % 2) * 4 + (s // 2) % 4
        return pl.ds(pl.multiple_of(place * OWN, OWN), OWN)

    def v_slot(b, s):
        return gathered.at[b, s // 8, v_rows(s), :]

    def v_copy(b, s, sem, to):
        return pltpu.make_async_remote_copy(
            src_ref=v_slot(b, s),
            dst_ref=v_slot(b, s),
            send_sem=sem,
            recv_sem=g_recv.at[b, s // 2],
            device_id=(to, col),
            device_id_type=MESH,
        )

    def share(b, m):
        s = same_core[m]
        return pltpu.make_async_remote_copy(
            src_ref=v_slot(b, s),
            dst_ref=v_slot(b, s),
            send_sem=f_send.at[b % 2, m],
            recv_sem=f_recv.at[b, s // 8],
            device_id=(mate, col),
            device_id_type=MESH,
        )

    def shared(b, z):
        half_slot = gathered.at[b, z, pl.ds(pl.multiple_of((1 - core) * 4 * OWN, OWN), 4 * OWN), :]
        pltpu.make_async_copy(half_slot, half_slot, f_recv.at[b, z]).wait()

    def start_gather(t, value):
        b, h = t % 4, t % 2
        gathered[b, zh, v_rows(row), :] = value
        for m in GATHER_ORDER:
            v_copy(b, row, g_send.at[h, m], same_core[m]).start()
        share(b, 0).start()

    def relay(b, m):
        return v_copy(b, same_core[4], r_send.at[m], same_core[m])

    for h in range(2):
        value = trial_ref[:, h * WIDTH : (h + 1) * WIDTH]
        current[h] = value.astype(jnp.float32)
        start_gather(h, value)
    previous[...] = jnp.zeros_like(previous)

    def h_copy(i, n, to):
        return pltpu.make_async_remote_copy(
            src_ref=h_ref.at[to, pl.ds(i * PIECE, PIECE)],
            dst_ref=hbuf.at[i, row],
            send_sem=h_send.at[i, n],
            recv_sem=h_recv.at[i],
            device_id=(to, col),
            device_id_type=MESH,
        )

    def h_own(i):
        return pltpu.make_async_copy(
            h_ref.at[row, pl.ds(i * PIECE, PIECE)], hbuf.at[i, row], h_recv.at[i]
        )

    def h_start(i, c):
        for n, step_to in enumerate(H_ORDER):
            h_copy(i, n, chip(*step_to)).start()
        h_own(i).start()
        return c

    lax.fori_loop(0, PIECES, h_start, 0)

    left = lax.broadcasted_iota(jnp.int32, (BLOCK, 2 * BLOCK), 1) < BLOCK

    def expand(piece, pair):
        even = (pair // 4) * 8 + (pair % 2) * 4 + (pair // 2) % 2
        odd = even + 2

        def one(at_piece, carry):
            i = piece * PIECE + at_piece

            def coef(s, q, j):
                return jnp.where(code_ref[(i * N_ROW + s) * PER + q] == j, 1.0, 0.0)

            def lanes(a, b):
                return jnp.where(left, a, b)

            be = hbuf[piece, even, at_piece].astype(jnp.float32)
            bo = hbuf[piece, odd, at_piece].astype(jnp.float32)
            re, ro = pltpu.roll(be, BLOCK, 1), pltpu.roll(bo, BLOCK, 1)
            first = be * lanes(coef(even, 0, 0), coef(even, 1, 1)) + re * lanes(
                coef(even, 1, 0), coef(even, 0, 1)
            )
            middle = jnp.where(
                left,
                be * coef(even, 0, 2) + re * coef(even, 1, 2),
                bo * coef(odd, 1, 0) + ro * coef(odd, 0, 0),
            )
            last = bo * lanes(coef(odd, 0, 1), coef(odd, 1, 2)) + ro * lanes(
                coef(odd, 1, 1), coef(odd, 0, 2)
            )
            at = pl.ds(pl.multiple_of(i * BLOCK, BLOCK), BLOCK)
            offset = (pair % 4) * (2 * OWN)
            for k, part in enumerate((first, middle, last)):
                dense[
                    pair // 4,
                    at,
                    pl.ds(pl.multiple_of(offset + k * 2 * BLOCK, 2 * BLOCK), 2 * BLOCK),
                ] = part.astype(jnp.bfloat16)
            return carry

        lax.fori_loop(0, PIECE, one, 0)

    def h_arrive(i, c):
        pltpu.make_async_copy(hbuf.at[i], hbuf.at[i], h_recv.at[i]).wait()

        def one_pair(pair, cc):
            expand(i, pair)
            return cc

        lax.fori_loop(0, N_ROW // 2, one_pair, 0)
        return c

    lax.fori_loop(0, PIECES, h_arrive, 0)

    def h_sent(i, c):
        for n, step_to in enumerate(H_ORDER):
            h_copy(i, n, chip(*step_to)).wait_send()
        return c

    lax.fori_loop(0, PIECES, h_sent, 0)

    center, half = center_ref[0], half_ref[0]
    HALF = ROWS // 2

    def p_copy(t, n):
        j, dl = SCATTER_ORDER[n]
        base = x if j < 2 else (x + 2) % 4
        to = (flip(base) if j % 2 else base) * 2 + (zl + dl) % 2
        return pltpu.make_async_remote_copy(
            src_ref=partial.at[t % 2, to],
            dst_ref=arrived.at[t % 4, col],
            send_sem=p_send.at[t % 2, n],
            recv_sem=p_recv.at[t % 4, col],
            device_id=(row, to),
            device_id_type=MESH,
        )

    def multiply(t, finish_other):
        b, h = t % 4, t % 2

        def product(chunk, rows_at):
            return jnp.dot(
                dense[chunk, rows_at, :],
                gathered[b, chunk],
                preferred_element_type=jnp.float32,
            )

        def arrive(m):
            v_copy(b, same_core[m], g_send.at[h, 1], mate).wait_recv()
            if m == 4:
                for n in RELAY_ORDER:
                    relay(b, n).start()
            share(b, m).start()

        def core_product(of_core, rows_at):
            k = pl.ds(pl.multiple_of(of_core * (CHUNK // 2), CHUNK // 2), CHUNK // 2)
            return jnp.dot(
                dense[1 - zh, rows_at, k],
                gathered[b, 1 - zh, k, :],
                preferred_element_type=jnp.float32,
            )

        for m in ARRIVAL_ORDER[:FINISH_AT]:
            arrive(m)
        shared(b, zh)
        total[...] = product(zh, slice(None))
        finish_other()
        for m in ARRIVAL_ORDER[FINISH_AT:]:
            arrive(m)
        total[...] += core_product(core, slice(None))
        shared(b, 1 - zh)

        for half_at, ready in enumerate(SCATTER_READY):
            first = (x // 2 + 1 + half_at) % 2
            at = pl.ds(pl.multiple_of(first * HALF, HALF), HALF)
            value = (total[at, :] + core_product(1 - core, at)).astype(jnp.bfloat16)
            partial[h, pl.ds(first * 4, 4)] = value.reshape(4, OWN, WIDTH)
            for n in ready:
                p_copy(t, n).start()

        for m in GATHER_ORDER:
            v_copy(b, row, g_send.at[h, m], mate).wait_send()
        for m in RELAY_ORDER:
            relay(b, m).wait_send()
        for m in range(CHIPS):
            share(b, m).wait_send()

    def finish(t):
        b, h = t % 4, t % 2
        arrived[b, col] = partial[h, col]
        for j in range(1, N_COL):
            s = (col + j) % N_COL
            pltpu.make_async_remote_copy(
                src_ref=partial.at[h, s],
                dst_ref=arrived.at[b, s],
                send_sem=p_send.at[h, 0],
                recv_sem=p_recv.at[b, s],
                device_id=(row, s),
                device_id_type=MESH,
            ).wait_recv()
        applied = arrived[b, 0].astype(jnp.float32)
        for s in range(1, N_COL):
            applied = applied + arrived[b, s].astype(jnp.float32)
        now = current[h]
        scale = jnp.where(t < 2, 1.0, 2.0)
        following = scale * (applied - center * now) / half - previous[h]
        previous[h] = now
        current[h] = following
        return following

    def scattered(t):
        for n in range(N_COL - 1):
            p_copy(t, n).wait_send()

    def turn(t, carry):
        def finish_other():
            @pl.when(t > 0)
            def _():
                following = finish(t - 1)

                @pl.when(t < TURNS - 1)
                def _():
                    start_gather(t + 1, following.astype(jnp.bfloat16))

                scattered(t - 1)

        multiply(t, finish_other)
        return carry

    lax.fori_loop(0, TURNS, turn, 0)
    finish(TURNS - 1)
    scattered(TURNS - 1)
    for h in range(2):
        out_ref[:, h * WIDTH : (h + 1) * WIDTH] = current[h]


def body(trial_vectors, h_blocks, block_col, block_count, center, half_width):
    slot = lax.broadcasted_iota(jnp.int32, (DOMAIN, N_ROW, PER), 2)
    filled = slot < block_count[0, 0][:, :, None]
    code = jnp.where(filled, block_col[0, 0], -1)
    vmem, smem, hbm = (
        pl.BlockSpec(memory_space=space) for space in (pltpu.VMEM, pltpu.SMEM, pl.ANY)
    )
    dma = pltpu.SemaphoreType.DMA
    bf16, f32 = jnp.bfloat16, jnp.float32
    return pl.pallas_call(
        kernel,
        out_shape=jax.ShapeDtypeStruct((OWN, VECTORS), f32),
        in_specs=[smem, smem, smem, hbm, hbm],
        out_specs=vmem,
        scratch_shapes=[
            pltpu.VMEM((OWN, VECTORS), bf16),
            dma,
            pltpu.VMEM((PIECES, N_ROW, PIECE, BLOCK, PER * BLOCK), bf16),
            pltpu.VMEM((2, ROWS, CHUNK), bf16),
            pltpu.VMEM((4, 2, CHUNK, WIDTH), bf16),
            pltpu.VMEM((ROWS, WIDTH), f32),
            pltpu.VMEM((2, N_COL, OWN, WIDTH), bf16),
            pltpu.VMEM((4, N_COL, OWN, WIDTH), bf16),
            pltpu.VMEM((2, OWN, WIDTH), f32),
            pltpu.VMEM((2, OWN, WIDTH), f32),
            dma((PIECES, N_ROW - 1)),
            dma((PIECES,)),
            dma((2, 5)),
            dma((4,)),
            dma((2, CHIPS)),
            dma((4, 2)),
            dma((4, CHIPS)),
            dma((2, N_COL - 1)),
            dma((4, N_COL)),
        ],
        compiler_params=pltpu.CompilerParams(
            collective_id=0, has_side_effects=True, vmem_limit_bytes=48 * 2**20
        ),
        name="filter",
    )(code.reshape(-1), center, half_width, trial_vectors, h_blocks[0, :, :, :, 0, :])


def solution(mesh):
    in_specs = (
        P(("row", "col"), None),
        P("col", None, None, None, "row", None),
        P("col", "row", None, None, None),
        P("col", "row", None, None),
        P(),
        P(),
    )
    out_specs = P(("row", "col"), None)
    return jax.shard_map(body, mesh=mesh, in_specs=in_specs, out_specs=out_specs, check_vma=False)
```
